32 devices in a mesh: ctx: 8 (over z, core), tp: 4 (over y, x).
Axes of the slice: x: 2, y: 2, z: 4, core: 2. Of those that a mesh axis runs over, the one named last changes fastest.
Arguments:
- queries: bfloat16 [16384, 1024], P(('ctx', 'tp')), may hold values from -6 to 6, as said below
- keys: bfloat16 [16384, 512], P(('ctx', 'tp')), may hold values from -9 to 9, as said below
- values: bfloat16 [16384, 512], P(('ctx', 'tp')), may hold values from -5 to 5
- output_gradient: bfloat16 [16384, 1024], P(('ctx', 'tp')), may hold values from -5 to 5
Outputs:
- attn_out: bfloat16 [16384, 1024], P(('ctx', 'tp'))
- grad_q: bfloat16 [16384, 1024], P(('ctx', 'tp'))
- grad_k: bfloat16 [16384, 512], P(('ctx', 'tp'))
- grad_v: bfloat16 [16384, 512], P(('ctx', 'tp'))
The draws below stay inside these ranges and needn't reach their ends.
Inputs may be any that keep to these rules, and one draw needn't show every extreme that they name: queries are real-valued. keys are real-valued.
All inputs are finite; a program needn't handle non-finite values.
Results may differ from the reference program's by a relative error of at most 0.023.
Values may be sent and summed in bfloat16 or wider, within the bound.
No kernel may reach another device: no remote copies, remote signals or barrier semaphores. Data moves between devices by JAX's collectives and lax.ppermute only.
A program may use at most 128 MiB of HBM per device.

```python
import jax
import jax.numpy as jnp
from jax import lax

HEAD_SIZE = 128
QUERY_GROUP = 2
WINDOW_LENGTH = 1024
QSCALE = 168
BLOCK = 512
KEY_VALUE_HEADS = 4
HQ = 8
SEQUENCE_TOKENS = 16384


def draw_queries(key, part):
    lowest_key_index = jax.random.fold_in(key, 1)
    final_output = jnp.clip(jax.random.normal(lowest_key_index, (SEQUENCE_TOKENS, HQ * HEAD_SIZE), jnp.float32), -3.0, 3.0)
    return final_output.astype(jnp.bfloat16)


def draw_keys(key, part):
    lowest_key_index = jax.random.fold_in(key, 2)
    spread_heads = jnp.exp(jax.random.uniform(jax.random.fold_in(key, 3), (SEQUENCE_TOKENS, 1), jnp.float32, jnp.log(0.3), jnp.log(3.0)))
    final_output = jnp.clip(jax.random.normal(lowest_key_index, (SEQUENCE_TOKENS, KEY_VALUE_HEADS * HEAD_SIZE), jnp.float32), -3.0, 3.0) * spread_heads
    return final_output.astype(jnp.bfloat16)


def level_of(rng, extent, cuts, smallest, high):
    loudness = 1.0
    for axis_at, blocks in cuts:
        draws = jax.random.uniform(jax.random.fold_in(jax.random.fold_in(rng, 6), axis_at), (blocks,), jnp.float32, smallest / len(cuts), high / len(cuts))
        loudness = loudness * jnp.repeat(jnp.exp(draws), extent[axis_at] // blocks).reshape((-1,) + (1,) * (len(extent) - 1 - axis_at))
    return loudness


def noise(rng, extent, deviation, limit, cuts=(), kind=jnp.bfloat16):
    result = deviation * jax.random.normal(rng, extent, jnp.float32)
    if cuts:
        result = result * level_of(rng, extent, cuts, -0.22, 0.18)
    return jnp.clip(result, -limit, limit).astype(kind)


def setup_inputs(seed: int = 0) -> dict:
    key_list = jax.random.split(jax.random.key(seed), 5)
    return {
        "queries": draw_queries(jax.random.fold_in(key_list[4], 71), 0),
        "keys": draw_keys(jax.random.fold_in(key_list[4], 71), 0),
        "values": noise(key_list[2], (SEQUENCE_TOKENS, KEY_VALUE_HEADS * HEAD_SIZE), 1.0, 5.0, ((0, 32),)),
        "output_gradient": noise(key_list[3], (SEQUENCE_TOKENS, HQ * HEAD_SIZE), 1.0, 5.0, ((0, 32),)),
    }


def band_mask(start, first):
    offsets = jnp.arange(BLOCK + WINDOW_LENGTH)[None, :] - jnp.arange(BLOCK)[:, None]
    inside = (offsets >= 1) & (offsets <= WINDOW_LENGTH)
    present = (start + jnp.arange(BLOCK + WINDOW_LENGTH) >= WINDOW_LENGTH) | first
    return (inside & present[None, :])[None]


def softmax_rows(logits, allowed):
    masked = jnp.where(allowed, logits, -jnp.inf)
    highest = jnp.max(masked, axis=-1, keepdims=True)
    raised = jnp.where(allowed, jnp.exp(masked - highest), 0.0)
    totals = jnp.sum(raised, axis=-1, keepdims=True)
    return raised / totals, highest, totals


def reference(queries, keys, values, output_gradient):
    scale = QSCALE ** -0.5
    window_span = BLOCK + WINDOW_LENGTH
    head_count = queries.reshape(SEQUENCE_TOKENS, KEY_VALUE_HEADS, QUERY_GROUP, HEAD_SIZE)
    gradient_tuple = output_gradient.reshape(SEQUENCE_TOKENS, KEY_VALUE_HEADS, QUERY_GROUP, HEAD_SIZE)
    padding_rows = jnp.zeros((WINDOW_LENGTH, KEY_VALUE_HEADS, HEAD_SIZE), jnp.bfloat16)
    key_extended = jnp.concatenate([padding_rows, keys.reshape(SEQUENCE_TOKENS, KEY_VALUE_HEADS, HEAD_SIZE)], 0)
    value_extended = jnp.concatenate([padding_rows, values.reshape(SEQUENCE_TOKENS, KEY_VALUE_HEADS, HEAD_SIZE)], 0)
    start_indices = jnp.arange(SEQUENCE_TOKENS // BLOCK, dtype=jnp.int32) * BLOCK

    def forward_pass(start):
        query_block = lax.dynamic_slice_in_dim(head_count, start, BLOCK, 0)
        key_block = lax.dynamic_slice_in_dim(key_extended, start, window_span, 0)
        value_block = lax.dynamic_slice_in_dim(value_extended, start, window_span, 0)
        allowed = band_mask(start, False)
        pieces = []
        for member in range(QUERY_GROUP):
            logits = jnp.einsum('bhd,lhd->hbl', query_block[:, :, member].astype(jnp.float32), key_block.astype(jnp.float32)) * scale
            probs = softmax_rows(logits, allowed)[0].astype(jnp.bfloat16)
            pieces.append(jnp.einsum('hbl,lhd->bhd', probs.astype(jnp.float32), value_block.astype(jnp.float32)))
        return jnp.stack(pieces, 2).astype(jnp.bfloat16)

    attended_output = lax.map(forward_pass, start_indices).reshape(SEQUENCE_TOKENS, KEY_VALUE_HEADS, QUERY_GROUP, HEAD_SIZE)
    delta = jnp.sum(gradient_tuple.astype(jnp.float32) * attended_output.astype(jnp.float32), -1)

    def backward(number, carry):
        key_gradient, value_gradient, query_grad = carry
        start = number * BLOCK
        query_block = lax.dynamic_slice_in_dim(head_count, start, BLOCK, 0)
        grad_block = lax.dynamic_slice_in_dim(gradient_tuple, start, BLOCK, 0)
        delta_block = lax.dynamic_slice_in_dim(delta, start, BLOCK, 0)
        key_block = lax.dynamic_slice_in_dim(key_extended, start, window_span, 0)
        value_block = lax.dynamic_slice_in_dim(value_extended, start, window_span, 0)
        allowed = band_mask(start, False)
        key_portion = jnp.zeros((window_span, KEY_VALUE_HEADS, HEAD_SIZE), jnp.float32)
        value_portion = jnp.zeros((window_span, KEY_VALUE_HEADS, HEAD_SIZE), jnp.float32)
        pieces = []
        for member in range(QUERY_GROUP):
            query_one = query_block[:, :, member].astype(jnp.float32)
            grad_one = grad_block[:, :, member].astype(jnp.float32)
            logits = jnp.einsum('bhd,lhd->hbl', query_one, key_block.astype(jnp.float32)) * scale
            probs = softmax_rows(logits, allowed)[0]
            probs_low = probs.astype(jnp.bfloat16).astype(jnp.float32)
            value_portion = value_portion + jnp.einsum('hbl,bhd->lhd', probs_low, grad_one)
            dprobs = jnp.einsum('bhd,lhd->hbl', grad_one, value_block.astype(jnp.float32))
            dlogits = (probs * (dprobs - delta_block[:, :, member].T[:, :, None])).astype(jnp.bfloat16).astype(jnp.float32)
            pieces.append((jnp.einsum('hbl,lhd->bhd', dlogits, key_block.astype(jnp.float32)) * scale).astype(jnp.bfloat16))
            key_portion = key_portion + jnp.einsum('hbl,bhd->lhd', dlogits, query_one) * scale
        query_grad = lax.dynamic_update_slice_in_dim(query_grad, jnp.stack(pieces, 2), start, 0)
        key_gradient = lax.dynamic_update_slice_in_dim(key_gradient, lax.dynamic_slice_in_dim(key_gradient, start, window_span, 0) + key_portion, start, 0)
        value_gradient = lax.dynamic_update_slice_in_dim(value_gradient, lax.dynamic_slice_in_dim(value_gradient, start, window_span, 0) + value_portion, start, 0)
        return key_gradient, value_gradient, query_grad

    starting_value = (jnp.zeros((SEQUENCE_TOKENS + WINDOW_LENGTH, KEY_VALUE_HEADS, HEAD_SIZE), jnp.float32), jnp.zeros((SEQUENCE_TOKENS + WINDOW_LENGTH, KEY_VALUE_HEADS, HEAD_SIZE), jnp.float32), jnp.zeros((SEQUENCE_TOKENS, KEY_VALUE_HEADS, QUERY_GROUP, HEAD_SIZE), jnp.bfloat16))
    key_gradient, value_gradient, query_grad = lax.fori_loop(0, SEQUENCE_TOKENS // BLOCK, backward, starting_value)
    return (attended_output.reshape(SEQUENCE_TOKENS, HQ * HEAD_SIZE), query_grad.reshape(SEQUENCE_TOKENS, HQ * HEAD_SIZE),
            key_gradient[WINDOW_LENGTH:].astype(jnp.bfloat16).reshape(SEQUENCE_TOKENS, KEY_VALUE_HEADS * HEAD_SIZE),
            value_gradient[WINDOW_LENGTH:].astype(jnp.bfloat16).reshape(SEQUENCE_TOKENS, KEY_VALUE_HEADS * HEAD_SIZE))
```

```python
import functools
import math

import jax
import jax.numpy as jnp
from jax import lax
from jax.experimental import pallas as pl
from jax.experimental.pallas import tpu as pltpu
from jax.sharding import PartitionSpec as P

HEAD_SIZE = 128
QUERY_GROUP = 2
WINDOW_LENGTH = 1024
QSCALE = 168
ROWS = 256
TILES = WINDOW_LENGTH // ROWS + 1
AXES = ("ctx", "tp")
LOW = -1e30


def nt(a, b):
    return lax.dot_general(a, b, (((1,), (1,)), ((), ())), preferred_element_type=jnp.float32)


def tn(a, b):
    return lax.dot_general(a, b, (((0,), (0,)), ((), ())), preferred_element_type=jnp.float32)


def stacked(ref):
    return jnp.concatenate(
        [ref[:, g * HEAD_SIZE : (g + 1) * HEAD_SIZE] for g in range(QUERY_GROUP)], 0
    )


def attention_kernel(pieces, steps, absent_ref, q_ref, g_ref, *refs):
    key_refs = refs[: 2 * len(pieces)]
    n_alias = len(refs) - 4 - 2 * len(pieces) * 2
    outs = refs[2 * len(pieces) :]
    o_ref, dq_ref = outs[0], outs[1]
    grad_refs = outs[2 : 2 + 2 * len(pieces)]
    kx, vx, dkx, dvx, s_scr, p_scr = outs[2 + 2 * len(pieces) :]
    scale = QSCALE**-0.5
    c = scale * math.log2(math.e)
    r = pl.program_id(1)

    def at(ref, start, size):
        return ref.at[start : start + size] if len(ref.shape) == 2 else ref.at[0, start : start + size]

    @pl.when(r == 0)
    def _():
        row = 0
        for n, size in enumerate(pieces):
            kx[row : row + size] = key_refs[2 * n][...].reshape(size, HEAD_SIZE)
            vx[row : row + size] = key_refs[2 * n + 1][...].reshape(size, HEAD_SIZE)
            row += size
        dkx[...] = jnp.zeros_like(dkx)
        dvx[...] = jnp.zeros_like(dvx)

    absent = absent_ref[0]
    base = pl.multiple_of(r * ROWS, ROWS)
    qs = stacked(q_ref)
    gs = stacked(g_ref)
    width = QUERY_GROUP * ROWS
    key_at = lax.broadcasted_iota(jnp.int32, (ROWS, width), 0)
    query_at = lax.broadcasted_iota(jnp.int32, (ROWS, width), 1) % ROWS
    upto = key_at <= query_at

    def rows(ref, t):
        return ref[pl.ds(base + t * ROWS, ROWS), :]

    top = jnp.full((1, width), LOW, jnp.float32)
    for t in range(TILES):
        s = nt(rows(kx, t), qs)
        if t == 0:
            s = jnp.where(upto, LOW, s)
        if t == TILES - 1:
            s = jnp.where(upto, s, LOW)
        s_scr[t] = s
        best = jnp.max(s, axis=0, keepdims=True)
        if t < TILES - 1:
            best = jnp.where(base + t * ROWS >= absent, best, LOW)
        top = jnp.maximum(top, best)
    top = top * c
    total = jnp.zeros((1, width), jnp.float32)
    out = jnp.zeros((HEAD_SIZE, width), jnp.float32)
    for t in range(TILES):
        lift = top if t == TILES - 1 else jnp.where(base + t * ROWS >= absent, top, -LOW)
        p = jnp.exp2(s_scr[t] * c - lift)
        total += jnp.sum(p, axis=0, keepdims=True)
        p_low = p.astype(jnp.bfloat16)
        p_scr[t] = p_low
        out += tn(rows(vx, t), p_low)
    inverse = 1.0 / total
    out_low = (out * inverse).astype(jnp.bfloat16).astype(jnp.float32)
    delta = jnp.sum(gs.astype(jnp.float32).T * out_low, axis=0, keepdims=True)
    out_rows = out_low.T.astype(jnp.bfloat16)
    column = jnp.broadcast_to(inverse, (HEAD_SIZE, width)).T
    q_part = (qs.astype(jnp.float32) * (column * scale)).astype(jnp.bfloat16)
    g_part = (gs.astype(jnp.float32) * column).astype(jnp.bfloat16)
    dq = jnp.zeros((HEAD_SIZE, width), jnp.float32)
    for t in range(TILES):
        here = pl.ds(base + t * ROWS, ROWS)
        p_low = p_scr[t]
        dp = nt(rows(vx, t), gs)
        ds = (p_low.astype(jnp.float32) * (dp - delta)).astype(jnp.bfloat16)
        dvx[here, :] += jnp.dot(p_low, g_part, preferred_element_type=jnp.float32)
        dkx[here, :] += jnp.dot(ds, q_part, preferred_element_type=jnp.float32)
        dq += tn(rows(kx, t), ds)
    dq_rows = (dq * (inverse * scale)).T.astype(jnp.bfloat16)
    for g in range(QUERY_GROUP):
        o_ref[:, g * HEAD_SIZE : (g + 1) * HEAD_SIZE] = out_rows[g * ROWS : (g + 1) * ROWS]
        dq_ref[:, g * HEAD_SIZE : (g + 1) * HEAD_SIZE] = dq_rows[g * ROWS : (g + 1) * ROWS]

    @pl.when(r == steps - 1)
    def _():
        row = 0
        for n, size in enumerate(pieces):
            for ref, wide in ((grad_refs[2 * n], dkx), (grad_refs[2 * n + 1], dvx)):
                ref[...] = wide[row : row + size].reshape(ref.shape).astype(ref.dtype)
            row += size


def flat_rows(width):
    return lambda spec: spec


def attention(absent, queries, grads, keys, values, before, head, heads, earlier):
    tokens = queries.shape[0]
    steps = tokens // ROWS
    group = QUERY_GROUP * HEAD_SIZE
    pieces = tuple(b.shape[2] for b in before) + (tokens,)
    wide = pl.BlockSpec((ROWS, group), lambda h, r: (r, head + h))
    own = pl.BlockSpec((tokens, HEAD_SIZE), lambda h, r: (0, head + h))

    def part(n, size):
        return pl.BlockSpec((1, 1, size, HEAD_SIZE), lambda h, r: (h, n, 0, 0))

    in_specs = [pl.BlockSpec(memory_space=pltpu.SMEM), wide, wide]
    args = [absent, queries, grads]
    out_specs = [wide, wide]
    out_shape = [jax.ShapeDtypeStruct(queries.shape, jnp.bfloat16)] * 2
    for b in before:
        size = b.shape[2]
        in_specs += [part(0, size), part(1, size)]
        args += [b, b]
        for n in range(2):
            out_specs.append(pl.BlockSpec((1, size, HEAD_SIZE), lambda h, r: (h, 0, 0)))
            out_shape.append(jax.ShapeDtypeStruct((heads, size, HEAD_SIZE), jnp.bfloat16))
    in_specs += [own, own]
    args += [keys, values]
    for n in range(2):
        out_specs.append(pl.BlockSpec((1, tokens, HEAD_SIZE), lambda h, r: (h, 0, 0)))
        out_shape.append(jax.ShapeDtypeStruct((heads, tokens, HEAD_SIZE), jnp.float32))
    extent = sum(pieces)
    width = QUERY_GROUP * ROWS
    aliases = {}
    body = functools.partial(attention_kernel, pieces, steps)
    if earlier is not None:
        n_in = len(args)
        in_specs += [pl.BlockSpec(memory_space=pl.ANY)] * 2
        args += list(earlier)
        aliases = {n_in: 0, n_in + 1: 1}
        inner = body

        def body(*refs):
            inner(*refs[:n_in], *refs[n_in + 2 :])

    pairs = heads * tokens * QUERY_GROUP * TILES * ROWS
    return pl.pallas_call(
        body,
        grid=(heads, steps),
        in_specs=in_specs,
        out_specs=out_specs,
        out_shape=out_shape,
        scratch_shapes=[
            pltpu.VMEM((extent, HEAD_SIZE), jnp.bfloat16),
            pltpu.VMEM((extent, HEAD_SIZE), jnp.bfloat16),
            pltpu.VMEM((extent, HEAD_SIZE), jnp.float32),
            pltpu.VMEM((extent, HEAD_SIZE), jnp.float32),
            pltpu.VMEM((TILES, ROWS, width), jnp.float32),
            pltpu.VMEM((TILES, ROWS, width), jnp.bfloat16),
        ],
        input_output_aliases=aliases,
        compiler_params=pltpu.CompilerParams(
            dimension_semantics=("arbitrary", "arbitrary"), vmem_limit_bytes=40 * 2**20
        ),
        cost_estimate=pl.CostEstimate(
            flops=24 * HEAD_SIZE * pairs, bytes_accessed=8 * 2**20 * heads // 4, transcendentals=pairs
        ),
        name="attention",
    )(*args)


def head_parts(keys, values, head, heads):
    rows = keys.shape[0]
    span = slice(head * HEAD_SIZE, (head + heads) * HEAD_SIZE)
    both = jnp.stack([keys[:, span], values[:, span]], 0).reshape(2, rows, heads, HEAD_SIZE)
    return both.transpose(2, 0, 1, 3)


def side_by_side(parts):
    return parts.transpose(1, 0, 2).reshape(parts.shape[1], -1)


CHUNKS = 4


def by_tokens(queries, keys, values, output_gradient):
    count = lax.axis_size(AXES)
    me = lax.axis_index(AXES)
    odd = me % 2 == 1
    rows = queries.shape[0]
    ahead = [(i, i + 2) for i in range(count - 2)]
    back = [(i + 2, i) for i in range(count - 2)]
    swap = [(i, i ^ 1) for i in range(count)]
    absent = jnp.maximum(WINDOW_LENGTH - me * rows, 0).astype(jnp.int32).reshape(1)
    kv_heads = keys.shape[1] // HEAD_SIZE
    heads = kv_heads // CHUNKS
    outs = None
    key_grads, value_grads = [], []
    starts = [h * heads for h in range(CHUNKS)]
    mine = [head_parts(keys, values, h, heads) for h in starts]
    far = [lax.ppermute(x, AXES, ahead) for x in mine]
    near = [lax.ppermute(jnp.where(odd, f, x), AXES, swap) for x, f in zip(mine, far)]
    for n, h in enumerate(starts):
        o, dq, fk, fv, nk, nv, ok, ov = attention(
            absent, queries, output_gradient, keys, values, (far[n], near[n]), h, heads, outs
        )
        outs = (o, dq)
        near_back = [lax.ppermute(x, AXES, swap) for x in (nk, nv)]
        relay = [jnp.where(odd, x.astype(jnp.float32) + y.astype(jnp.float32), x.astype(jnp.float32)).astype(jnp.bfloat16) for x, y in zip((fk, fv), near_back)]
        far_back = [lax.ppermute(x, AXES, back) for x in relay]
        for own, x, y, grads in zip((ok, ov), near_back, far_back, (key_grads, value_grads)):
            total = own + y.astype(jnp.float32) + jnp.where(odd, 0.0, x.astype(jnp.float32))
            grads.append(side_by_side(total.astype(jnp.bfloat16)))
    return (*outs, jnp.concatenate(key_grads, 1), jnp.concatenate(value_grads, 1))


def by_heads(queries, keys, values, output_gradient):
    tp = lax.axis_size("tp")
    ctx = lax.axis_size("ctx")

    def gathered(x):
        return lax.all_to_all(x, "tp", split_axis=1, concat_axis=0, tiled=True)

    def returned(x):
        return lax.all_to_all(x, "tp", split_axis=0, concat_axis=1, tiled=True)

    queries, keys, values, grads = map(gathered, (queries, keys, values, output_gradient))
    rows = queries.shape[0]
    kv_heads = keys.shape[1] // HEAD_SIZE
    tail = head_parts(keys[rows - WINDOW_LENGTH :], values[rows - WINDOW_LENGTH :], 0, kv_heads)
    rim = lax.ppermute(tail, "ctx", [(i, i + 1) for i in range(ctx - 1)])
    first = lax.axis_index("ctx") == 0
    absent = jnp.where(first, WINDOW_LENGTH, 0).astype(jnp.int32).reshape(1)
    o, dq, fk, fv, ok, ov = attention(
        absent, queries, grads, keys, values, (rim,), 0, kv_heads, None
    )
    results = [o, dq]
    for own, rim_grad in ((ok, fk), (ov, fv)):
        back = lax.ppermute(rim_grad, "ctx", [(i + 1, i) for i in range(ctx - 1)])
        own = own.at[:, rows - WINDOW_LENGTH :].add(back.astype(jnp.float32))
        results.append(side_by_side(own.astype(jnp.bfloat16)))
    return tuple(map(returned, results))


def on_device(queries, keys, values, output_gradient):
    rows = queries.shape[0]
    if 2 * rows == WINDOW_LENGTH and lax.axis_size(AXES) % 2 == 0:
        return by_tokens(queries, keys, values, output_gradient)
    return by_heads(queries, keys, values, output_gradient)


def solution(mesh):
    spec = P(AXES, None)
    return jax.shard_map(
        on_device, mesh=mesh, in_specs=(spec,) * 4, out_specs=(spec,) * 4, check_vma=False
    )
```

```python
import functools
import math

import jax
import jax.numpy as jnp
from jax import lax
from jax.experimental import pallas as pl
from jax.experimental.pallas import tpu as pltpu
from jax.sharding import PartitionSpec as P

HEAD_SIZE = 128
QUERY_GROUP = 2
WINDOW_LENGTH = 1024
QSCALE = 168
BLOCK = 512
ROWS = 256
TILES = WINDOW_LENGTH // ROWS + 1
AXES = ("ctx", "tp")
LOW = -1e30


def nt(a, b):
    return lax.dot_general(a, b, (((1,), (1,)), ((), ())), preferred_element_type=jnp.float32)


def tn(a, b):
    return lax.dot_general(a, b, (((0,), (0,)), ((), ())), preferred_element_type=jnp.float32)


def attention_kernel(tokens, absent_ref, q_ref, g_ref, *refs):
    pieces = WINDOW_LENGTH // tokens + 1
    o_ref, dq_ref = refs[2 * pieces], refs[2 * pieces + 1]
    grad_refs = refs[2 * pieces + 2 : 3 * pieces + 2]
    s_scr, p_scr, d_scr, kt_scr, vt_scr, dkt_scr, dvt_scr = refs[3 * pieces + 2 :]
    scale = QSCALE**-0.5
    c = scale * math.log2(math.e)
    steps = tokens // ROWS
    width = QUERY_GROUP * ROWS
    span = TILES * ROWS
    absent = absent_ref[0]
    key_at = lax.broadcasted_iota(jnp.int32, (ROWS, ROWS), 0)
    query_at = lax.broadcasted_iota(jnp.int32, (ROWS, ROWS), 1)
    upto = key_at <= query_at

    def piece(which, n):
        ref = refs[2 * n + which]
        return ref[...].reshape(ref.shape[-2:])

    def tile(which, e):
        ref = refs[2 * (e // steps) + which]
        start = e % steps * ROWS
        if len(ref.shape) == 2:
            return ref[start : start + ROWS, :]
        return ref[0, 0, start : start + ROWS, :]

    def stacked(ref, r):
        return jnp.concatenate(
            [ref[r * ROWS : (r + 1) * ROWS, g * HEAD_SIZE : (g + 1) * HEAD_SIZE] for g in range(QUERY_GROUP)], 0
        )

    def unstacked(ref, r, x):
        for g in range(QUERY_GROUP):
            ref[r * ROWS : (r + 1) * ROWS, g * HEAD_SIZE : (g + 1) * HEAD_SIZE] = x[g * ROWS : (g + 1) * ROWS]

    def eights(x, op):
        return op(x.reshape(ROWS // 8, 8, ROWS), axis=0)

    for n in range(pieces):
        kt_scr[:, n * tokens : (n + 1) * tokens] = piece(0, n).T
        vt_scr[:, n * tokens : (n + 1) * tokens] = piece(1, n).T

    groups = range(QUERY_GROUP)

    def part(r):
        q_t, g_t = stacked(q_ref, r).T, stacked(g_ref, r).T
        cols = [slice(g * ROWS, (g + 1) * ROWS) for g in groups]
        tops = [jnp.full((8, ROWS), LOW, jnp.float32) for g in groups]
        for t in range(TILES):
            for g in groups:
                s = jnp.dot(tile(0, r + t), q_t[:, cols[g]], preferred_element_type=jnp.float32)
                if t == 0:
                    s = jnp.where(upto, LOW, s)
                if t == TILES - 1:
                    s = jnp.where(upto, s, LOW)
                s_scr[r, g, t] = s
                best = eights(s, jnp.max)
                if t < TILES - 1:
                    best = jnp.where((r + t) * ROWS >= absent, best, LOW)
                tops[g] = jnp.maximum(tops[g], best)
            yield
        tops = [jnp.max(x, axis=0, keepdims=True) * c for x in tops]
        totals = [jnp.zeros((8, ROWS), jnp.float32) for g in groups]
        for t in range(TILES):
            for g in groups:
                lift = tops[g] if t == TILES - 1 else jnp.where((r + t) * ROWS >= absent, tops[g], -LOW)
                p = jnp.exp2(s_scr[r, g, t] * c - lift)
                totals[g] += eights(p, jnp.sum)
                p_scr[r, t * ROWS : (t + 1) * ROWS, cols[g]] = p.astype(jnp.bfloat16)
            yield
        inverse = 1.0 / jnp.concatenate([jnp.sum(x, axis=0, keepdims=True) for x in totals], 1)
        out = jnp.dot(vt_scr[:, r * ROWS : r * ROWS + span], p_scr[r], preferred_element_type=jnp.float32)
        out_low = (out * inverse).astype(jnp.bfloat16)
        delta = jnp.sum(g_t.astype(jnp.float32) * out_low.astype(jnp.float32), axis=0, keepdims=True)
        unstacked(o_ref, r, out_low.T)
        q_part = (q_t.astype(jnp.float32) * (inverse * scale)).astype(jnp.bfloat16)
        g_part = (g_t.astype(jnp.float32) * inverse).astype(jnp.bfloat16)
        for t in range(TILES):
            for g in groups:
                dp = jnp.dot(tile(1, r + t), g_t[:, cols[g]], preferred_element_type=jnp.float32)
                here = slice(t * ROWS, (t + 1) * ROWS)
                p = p_scr[r, here, cols[g]].astype(jnp.float32)
                d_scr[r, here, cols[g]] = (p * (dp - delta[:, cols[g]])).astype(jnp.bfloat16)
            add(dvt_scr, nt(g_part, p_scr[r, here, :]), r, t)
            yield
        dq = jnp.dot(kt_scr[:, r * ROWS : r * ROWS + span], d_scr[r], preferred_element_type=jnp.float32)
        unstacked(dq_ref, r, (dq * (inverse * scale)).astype(jnp.bfloat16).T)
        for t in range(TILES):
            add(dkt_scr, nt(q_part, d_scr[r, t * ROWS : (t + 1) * ROWS, :]), r, t)
        yield

    def add(scr, x, r, t):
        here = slice((r + t) * ROWS, (r + t + 1) * ROWS)
        scr[:, here] = x if r == 0 or t == TILES - 1 else scr[:, here] + x

    running = [part(r) for r in range(steps)]
    for r in ORDER(steps):
        next(running[r], None)
    for n in range(pieces):
        for k, scr in enumerate((dkt_scr, dvt_scr)):
            grad_refs[n][0, k] = scr[:, n * tokens : (n + 1) * tokens].T.astype(grad_refs[n].dtype)


def in_turn(steps):
    return [r for r in range(steps) for _ in range(3 * TILES + 1)]


def staggered(steps):
    turns = []
    for stage in range(steps + 3):
        for _ in range(TILES + (stage >= 3)):
            turns += [r for r in range(steps) if 0 <= stage - r < 4]
    return turns


ORDER = staggered


def attention(absent, queries, grads, keys, values, before, head, heads, earlier):
    tokens = queries.shape[0]
    group = QUERY_GROUP * HEAD_SIZE
    wide = pl.BlockSpec((tokens, group), lambda h: (0, head + h))
    own = pl.BlockSpec((tokens, HEAD_SIZE), lambda h: (0, head + h))

    def part(n):
        return pl.BlockSpec((1, 1, tokens, HEAD_SIZE), lambda h: (h, n, 0, 0))

    in_specs = [pl.BlockSpec(memory_space=pltpu.SMEM), wide, wide]
    args = [absent, queries, grads]
    out_specs = [wide, wide]
    out_shape = [jax.ShapeDtypeStruct(queries.shape, jnp.bfloat16)] * 2
    for b in before:
        in_specs += [part(0), part(1)]
        args += [b, b]
    in_specs += [own, own]
    args += [keys, values]
    for kind in [jnp.bfloat16] * len(before) + [jnp.float32]:
        out_specs.append(pl.BlockSpec((1, 2, tokens, HEAD_SIZE), lambda h: (h, 0, 0, 0)))
        out_shape.append(jax.ShapeDtypeStruct((heads, 2, tokens, HEAD_SIZE), kind))
    width = QUERY_GROUP * ROWS
    extent = WINDOW_LENGTH + tokens
    steps = tokens // ROWS
    aliases = {}
    body = functools.partial(attention_kernel, tokens)
    if earlier is not None:
        n_in = len(args)
        in_specs += [pl.BlockSpec(memory_space=pl.ANY)] * 2
        args += list(earlier)
        aliases = {n_in: 0, n_in + 1: 1}
        inner = body

        def body(*refs):
            inner(*refs[:n_in], *refs[n_in + 2 :])

    pairs = heads * tokens * QUERY_GROUP * TILES * ROWS
    return pl.pallas_call(
        body,
        grid=(heads,),
        in_specs=in_specs,
        out_specs=out_specs,
        out_shape=out_shape,
        scratch_shapes=[
            pltpu.VMEM((steps, QUERY_GROUP, TILES, ROWS, ROWS), jnp.float32),
            pltpu.VMEM((steps, TILES * ROWS, width), jnp.bfloat16),
            pltpu.VMEM((steps, TILES * ROWS, width), jnp.bfloat16),
            pltpu.VMEM((HEAD_SIZE, extent), jnp.bfloat16),
            pltpu.VMEM((HEAD_SIZE, extent), jnp.bfloat16),
            pltpu.VMEM((HEAD_SIZE, extent), jnp.float32),
            pltpu.VMEM((HEAD_SIZE, extent), jnp.float32),
        ],
        input_output_aliases=aliases,
        compiler_params=pltpu.CompilerParams(
            dimension_semantics=("arbitrary",), vmem_limit_bytes=26 * 2**20
        ),
        cost_estimate=pl.CostEstimate(
            flops=12 * HEAD_SIZE * pairs, bytes_accessed=2 * 2**20 * heads, transcendentals=0
        ),
        name="attention",
    )(*args)


def head_parts(keys, values, head, heads):
    rows = keys.shape[0]
    span = slice(head * HEAD_SIZE, (head + heads) * HEAD_SIZE)
    both = jnp.stack([keys[:, span], values[:, span]], 0).reshape(2, rows, heads, HEAD_SIZE)
    return both.transpose(2, 0, 1, 3)


def side_by_side(parts):
    return parts.transpose(1, 0, 2).reshape(parts.shape[1], -1)


def after(x, *others):
    return lax.optimization_barrier((x, *others))[0] if others else x


def wide(x):
    return x.astype(jnp.float32)


CHUNKS = 4


def by_tokens(queries, keys, values, output_gradient):
    count = lax.axis_size(AXES)
    me = lax.axis_index(AXES)
    odd = me % 2 == 1
    rows = queries.shape[0]
    ahead = [(i, (i + 2) % count) for i in range(count)]
    back = [((i + 2) % count, i) for i in range(count)]
    swap = [(i, i ^ 1) for i in range(count)]
    absent = jnp.maximum(WINDOW_LENGTH - me * rows, 0).astype(jnp.int32).reshape(1)
    kv_heads = keys.shape[1] // HEAD_SIZE
    heads = kv_heads // CHUNKS
    far, send, near, relay, near_back, far_back, own = ({} for _ in range(7))
    mine = [head_parts(keys, values, n * heads, heads) for n in range(CHUNKS)]

    held = {n: () for n in range(CHUNKS)}

    def fetch_far(n):
        block = after(mine[n], *held[n])
        far[n] = lax.ppermute(block, AXES, ahead)

    def fetch_near(n):
        send[n] = jnp.where(odd, far[n], mine[n])
        near[n] = lax.ppermute(send[n], AXES, swap)

    def give_near(n):
        near_back[n] = lax.ppermute(to_near[n], AXES, swap)

    def give_far(n):
        relay[n] = jnp.where(odd, wide(to_far[n]) + wide(near_back[n]), wide(to_far[n])).astype(jnp.bfloat16)
        far_back[n] = lax.ppermute(relay[n], AXES, back)

    outs = None
    to_far, to_near = {}, {}

    def compute(n, *waits):
        nonlocal outs
        o, dq, to_far[n], to_near[n], own[n] = attention(
            after(absent, *waits), queries, output_gradient, keys, values, (far[n], near[n]), n * heads, heads, outs
        )
        outs = (o, dq)

    fetch_far(0)
    fetch_far(1)
    fetch_near(0)
    held[2] = (send[0],)
    fetch_far(2)
    fetch_near(1)
    held[3] = (far[1],)
    fetch_far(3)
    compute(0, send[1])
    give_near(0)
    far[2] = after(far[2], to_far[0])
    fetch_near(2)
    compute(1, send[2])
    give_near(1)
    far[3] = after(far[3], to_far[1])
    fetch_near(3)
    compute(2, send[3])
    give_near(2)
    near_back[0] = after(near_back[0], to_far[2])
    give_far(0)
    compute(3, relay[0])
    give_near(3)
    near_back[1] = after(near_back[1], to_far[3])
    give_far(1)
    give_far(2)
    give_far(3)
    key_grads, value_grads = [], []
    for n in range(CHUNKS):
        total = own[n] + wide(far_back[n]) + jnp.where(odd, 0.0, wide(near_back[n]))
        total = total.astype(jnp.bfloat16)
        for k, parts in enumerate((key_grads, value_grads)):
            parts += [total[h, k] for h in range(heads)]
    return (*outs, jnp.concatenate(key_grads, 1), jnp.concatenate(value_grads, 1))


def by_heads(queries, keys, values, output_gradient):
    tp = lax.axis_size("tp")
    ctx = lax.axis_size("ctx")

    def gathered(x):
        return lax.all_to_all(x, "tp", split_axis=1, concat_axis=0, tiled=True)

    def returned(x):
        return lax.all_to_all(x, "tp", split_axis=0, concat_axis=1, tiled=True)

    queries, keys, values, grads = map(gathered, (queries, keys, values, output_gradient))
    rows = queries.shape[0]
    kv_heads = keys.shape[1] // HEAD_SIZE
    tail = head_parts(keys[rows - WINDOW_LENGTH :], values[rows - WINDOW_LENGTH :], 0, kv_heads)
    rim = lax.ppermute(tail, "ctx", [(i, i + 1) for i in range(ctx - 1)])
    absent = jnp.where(lax.axis_index("ctx") == 0, WINDOW_LENGTH, 0).astype(jnp.int32)
    both = jnp.concatenate([rim, head_parts(keys, values, 0, kv_heads)], 2)
    both_grads = jnp.zeros(both.shape, jnp.float32)
    outs, query_grads = [], []
    for start in range(0, rows, BLOCK):
        here = slice(start, start + BLOCK)
        before = [both[:, :, at : at + BLOCK] for at in range(start, start + WINDOW_LENGTH, BLOCK)]
        o, dq, *parts = attention(
            jnp.maximum(absent - start, 0).reshape(1), queries[here], grads[here], keys[here], values[here],
            before, 0, kv_heads, None,
        )
        outs.append(o)
        query_grads.append(dq)
        for n, x in enumerate(parts):
            at = start + n * BLOCK
            both_grads = both_grads.at[:, :, at : at + BLOCK].add(wide(x))
    back = lax.ppermute(both_grads[:, :, :WINDOW_LENGTH], "ctx", [(i + 1, i) for i in range(ctx - 1)])
    own = both_grads[:, :, WINDOW_LENGTH:]
    own = own.at[:, :, rows - WINDOW_LENGTH :].add(back).astype(jnp.bfloat16)
    results = (jnp.concatenate(outs), jnp.concatenate(query_grads), side_by_side(own[:, 0]), side_by_side(own[:, 1]))
    return tuple(map(returned, results))


def on_device(queries, keys, values, output_gradient):
    rows = queries.shape[0]
    if 2 * rows == WINDOW_LENGTH and lax.axis_size(AXES) % 2 == 0:
        return by_tokens(queries, keys, values, output_gradient)
    return by_heads(queries, keys, values, output_gradient)


def solution(mesh):
    spec = P(AXES, None)
    return jax.shard_map(
        on_device, mesh=mesh, in_specs=(spec,) * 4, out_specs=(spec,) * 4, check_vma=False
    )
```

```python
import functools
import math

import jax
import jax.numpy as jnp
from jax import lax
from jax.experimental import pallas as pl
from jax.experimental.pallas import tpu as pltpu
from jax.sharding import PartitionSpec as P

HEAD_SIZE = 128
QUERY_GROUP = 2
WINDOW_LENGTH = 1024
QSCALE = 168
BLOCK = 512
ROWS = 256
TILES = WINDOW_LENGTH // ROWS + 1
AXES = ("ctx", "tp")
LOW = -1e30


def nt(a, b):
    return lax.dot_general(a, b, (((1,), (1,)), ((), ())), preferred_element_type=jnp.float32)


def tn(a, b):
    return lax.dot_general(a, b, (((0,), (0,)), ((), ())), preferred_element_type=jnp.float32)


def attention_kernel(tokens, absent_ref, q_ref, g_ref, *refs):
    pieces = WINDOW_LENGTH // tokens + 1
    o_ref, dq_ref = refs[2 * pieces], refs[2 * pieces + 1]
    grad_refs = refs[2 * pieces + 2 : 3 * pieces + 2]
    s_scr, p_scr, d_scr, kt_scr, vt_scr, dkt_scr, dvt_scr = refs[3 * pieces + 2 :]
    scale = QSCALE**-0.5
    c = scale * math.log2(math.e)
    steps = tokens // ROWS
    width = QUERY_GROUP * ROWS
    span = TILES * ROWS
    absent = absent_ref[0]
    key_at = lax.broadcasted_iota(jnp.int32, (ROWS, ROWS), 0)
    query_at = lax.broadcasted_iota(jnp.int32, (ROWS, ROWS), 1)
    upto = key_at <= query_at

    def piece(which, n):
        ref = refs[2 * n + which]
        return ref[...].reshape(ref.shape[-2:])

    def tile(which, e):
        ref = refs[2 * (e // steps) + which]
        start = e % steps * ROWS
        if len(ref.shape) == 2:
            return ref[start : start + ROWS, :]
        return ref[0, 0, start : start + ROWS, :]

    def stacked(ref, r):
        return jnp.concatenate(
            [ref[r * ROWS : (r + 1) * ROWS, g * HEAD_SIZE : (g + 1) * HEAD_SIZE] for g in range(QUERY_GROUP)], 0
        )

    def unstacked(ref, r, x):
        for g in range(QUERY_GROUP):
            ref[r * ROWS : (r + 1) * ROWS, g * HEAD_SIZE : (g + 1) * HEAD_SIZE] = x[g * ROWS : (g + 1) * ROWS]

    def eights(x, op):
        return op(x.reshape(ROWS // 8, 8, ROWS), axis=0)

    for n in range(pieces):
        kt_scr[:, n * tokens : (n + 1) * tokens] = piece(0, n).T
        vt_scr[:, n * tokens : (n + 1) * tokens] = piece(1, n).T

    groups = range(QUERY_GROUP)

    def part(r):
        q_t, g_t = stacked(q_ref, r).T, stacked(g_ref, r).T
        cols = [slice(g * ROWS, (g + 1) * ROWS) for g in groups]
        tops = [jnp.full((8, ROWS), LOW, jnp.float32) for g in groups]
        for t in range(TILES):
            for g in groups:
                s = jnp.dot(tile(0, r + t), q_t[:, cols[g]], preferred_element_type=jnp.float32)
                if t == 0:
                    s = jnp.where(upto, LOW, s)
                if t == TILES - 1:
                    s = jnp.where(upto, s, LOW)
                s_scr[r, g, t] = s
                best = eights(s, jnp.max)
                if t < TILES - 1:
                    best = jnp.where((r + t) * ROWS >= absent, best, LOW)
                tops[g] = jnp.maximum(tops[g], best)
            yield
        tops = [jnp.max(x, axis=0, keepdims=True) * c for x in tops]
        totals = [jnp.zeros((8, ROWS), jnp.float32) for g in groups]
        for t in range(TILES):
            for g in groups:
                lift = tops[g] if t == TILES - 1 else jnp.where((r + t) * ROWS >= absent, tops[g], -LOW)
                p = jnp.exp2(s_scr[r, g, t] * c - lift)
                totals[g] += eights(p, jnp.sum)
                p_scr[r, t * ROWS : (t + 1) * ROWS, cols[g]] = p.astype(jnp.bfloat16)
            yield
        inverse = 1.0 / jnp.concatenate([jnp.sum(x, axis=0, keepdims=True) for x in totals], 1)
        out = jnp.dot(vt_scr[:, r * ROWS : r * ROWS + span], p_scr[r], preferred_element_type=jnp.float32)
        out_low = (out * inverse).astype(jnp.bfloat16)
        delta = jnp.sum(g_t.astype(jnp.float32) * out_low.astype(jnp.float32), axis=0, keepdims=True)
        unstacked(o_ref, r, out_low.T)
        q_part = (q_t.astype(jnp.float32) * (inverse * scale)).astype(jnp.bfloat16)
        g_part = (g_t.astype(jnp.float32) * inverse).astype(jnp.bfloat16)
        for t in range(TILES):
            for g in groups:
                dp = jnp.dot(tile(1, r + t), g_t[:, cols[g]], preferred_element_type=jnp.float32)
                here = slice(t * ROWS, (t + 1) * ROWS)
                p = p_scr[r, here, cols[g]].astype(jnp.float32)
                d_scr[r, here, cols[g]] = (p * (dp - delta[:, cols[g]])).astype(jnp.bfloat16)
            add(dvt_scr, nt(g_part, p_scr[r, here, :]), r, t)
            yield
        dq = jnp.dot(kt_scr[:, r * ROWS : r * ROWS + span], d_scr[r], preferred_element_type=jnp.float32)
        unstacked(dq_ref, r, (dq * (inverse * scale)).astype(jnp.bfloat16).T)
        for t in range(TILES):
            add(dkt_scr, nt(q_part, d_scr[r, t * ROWS : (t + 1) * ROWS, :]), r, t)
        yield

    def add(scr, x, r, t):
        here = slice((r + t) * ROWS, (r + t + 1) * ROWS)
        scr[:, here] = x if r == 0 or t == TILES - 1 else scr[:, here] + x

    running = [part(r) for r in range(steps)]
    for r in ORDER(steps):
        next(running[r], None)
    for n in range(pieces):
        for k, scr in enumerate((dkt_scr, dvt_scr)):
            grad_refs[n][0, k] = scr[:, n * tokens : (n + 1) * tokens].T.astype(grad_refs[n].dtype)


def in_turn(steps):
    return [r for r in range(steps) for _ in range(3 * TILES + 1)]


def staggered(steps):
    turns = []
    for stage in range(steps + 3):
        for _ in range(TILES + (stage >= 3)):
            turns += [r for r in range(steps) if 0 <= stage - r < 4]
    return turns


ORDER = staggered


def attention(absent, queries, grads, keys, values, before, head, heads, earlier):
    tokens = queries.shape[0]
    group = QUERY_GROUP * HEAD_SIZE
    wide = pl.BlockSpec((tokens, group), lambda h: (0, head + h))
    own = pl.BlockSpec((tokens, HEAD_SIZE), lambda h: (0, head + h))

    def part(n):
        return pl.BlockSpec((1, 1, tokens, HEAD_SIZE), lambda h: (h, n, 0, 0))

    in_specs = [pl.BlockSpec(memory_space=pltpu.SMEM), wide, wide]
    args = [absent, queries, grads]
    out_specs = [wide, wide]
    out_shape = [jax.ShapeDtypeStruct(queries.shape, jnp.bfloat16)] * 2
    for b in before:
        in_specs += [part(0), part(1)]
        args += [b, b]
    in_specs += [own, own]
    args += [keys, values]
    for kind in [jnp.bfloat16] * len(before) + [jnp.float32]:
        out_specs.append(pl.BlockSpec((1, 2, tokens, HEAD_SIZE), lambda h: (h, 0, 0, 0)))
        out_shape.append(jax.ShapeDtypeStruct((heads, 2, tokens, HEAD_SIZE), kind))
    width = QUERY_GROUP * ROWS
    extent = WINDOW_LENGTH + tokens
    steps = tokens // ROWS
    aliases = {}
    body = functools.partial(attention_kernel, tokens)
    if earlier is not None:
        n_in = len(args)
        in_specs += [pl.BlockSpec(memory_space=pl.ANY)] * 2
        args += list(earlier)
        aliases = {n_in: 0, n_in + 1: 1}
        inner = body

        def body(*refs):
            inner(*refs[:n_in], *refs[n_in + 2 :])

    pairs = heads * tokens * QUERY_GROUP * TILES * ROWS
    return pl.pallas_call(
        body,
        grid=(heads,),
        in_specs=in_specs,
        out_specs=out_specs,
        out_shape=out_shape,
        scratch_shapes=[
            pltpu.VMEM((steps, QUERY_GROUP, TILES, ROWS, ROWS), jnp.float32),
            pltpu.VMEM((steps, TILES * ROWS, width), jnp.bfloat16),
            pltpu.VMEM((steps, TILES * ROWS, width), jnp.bfloat16),
            pltpu.VMEM((HEAD_SIZE, extent), jnp.bfloat16),
            pltpu.VMEM((HEAD_SIZE, extent), jnp.bfloat16),
            pltpu.VMEM((HEAD_SIZE, extent), jnp.float32),
            pltpu.VMEM((HEAD_SIZE, extent), jnp.float32),
        ],
        input_output_aliases=aliases,
        compiler_params=pltpu.CompilerParams(
            dimension_semantics=("arbitrary",), vmem_limit_bytes=26 * 2**20
        ),
        cost_estimate=pl.CostEstimate(
            flops=12 * HEAD_SIZE * pairs, bytes_accessed=2 * 2**20 * heads, transcendentals=0
        ),
        name="attention",
    )(*args)


def head_parts(keys, values, head, heads):
    rows = keys.shape[0]
    span = slice(head * HEAD_SIZE, (head + heads) * HEAD_SIZE)
    if heads == 1:
        return jnp.stack([lax.optimization_barrier(keys[:, span]), lax.optimization_barrier(values[:, span])], 0)[None]
    both = jnp.stack([keys[:, span], values[:, span]], 0).reshape(2, rows, heads, HEAD_SIZE)
    return both.transpose(2, 0, 1, 3)


def side_by_side(parts):
    return parts.transpose(1, 0, 2).reshape(parts.shape[1], -1)


def after(x, *others):
    return lax.optimization_barrier((x, *others))[0] if others else x


def wide(x):
    return x.astype(jnp.float32)


CHUNKS = 4


def by_tokens(queries, keys, values, output_gradient):
    count = lax.axis_size(AXES)
    me = lax.axis_index(AXES)
    odd = me % 2 == 1
    rows = queries.shape[0]
    ahead = [(i, (i + 2) % count) for i in range(count)]
    back = [((i + 2) % count, i) for i in range(count)]
    swap = [(i, i ^ 1) for i in range(count)]
    absent = jnp.maximum(WINDOW_LENGTH - me * rows, 0).astype(jnp.int32).reshape(1)
    kv_heads = keys.shape[1] // HEAD_SIZE
    heads = kv_heads // CHUNKS
    far, send, near, relay, near_back, far_back, own = ({} for _ in range(7))
    mine = [head_parts(keys, values, n * heads, heads) for n in range(CHUNKS)]

    held = {n: () for n in range(CHUNKS)}

    def fetch_far(n):
        block = after(mine[n], *held[n])
        far[n] = lax.ppermute(block, AXES, ahead)

    def fetch_near(n):
        send[n] = jnp.where(odd, far[n], mine[n])
        near[n] = lax.ppermute(send[n], AXES, swap)

    def give_near(n):
        near_back[n] = lax.ppermute(to_near[n], AXES, swap)

    def give_far(n):
        if n > 0:
            near_back[n] = after(near_back[n], relay[n - 1])
        relay[n] = jnp.where(odd, wide(to_far[n]) + wide(near_back[n]), wide(to_far[n])).astype(jnp.bfloat16)
        far_back[n] = lax.ppermute(relay[n], AXES, back)

    outs = None
    to_far, to_near = {}, {}

    def compute(n, *waits):
        nonlocal outs
        o, dq, to_far[n], to_near[n], own[n] = attention(
            after(absent, *waits), queries, output_gradient, keys, values, (far[n], near[n]), n * heads, heads, outs
        )
        outs = (o, dq)

    fetch_far(0)
    fetch_far(1)
    fetch_near(0)
    held[2] = (send[0],)
    fetch_far(2)
    fetch_near(1)
    held[3] = (send[1],)
    fetch_far(3)
    compute(0, send[1])
    give_near(0)
    far[2] = after(far[2], to_far[0])
    fetch_near(2)
    compute(1, send[2])
    far[3] = after(far[3], to_far[1])
    fetch_near(3)
    compute(2, send[3])
    to_near[1] = after(to_near[1], to_far[2])
    give_near(1)
    give_near(2)
    near_back[0] = after(near_back[0], to_far[2])
    give_far(0)
    compute(3, relay[0])
    give_near(3)
    near_back[1] = after(near_back[1], to_far[3])
    give_far(1)
    give_far(2)
    give_far(3)
    key_grads, value_grads = [], []
    for n in range(CHUNKS):
        total = own[n] + wide(far_back[n]) + jnp.where(odd, 0.0, wide(near_back[n]))
        total = total.astype(jnp.bfloat16)
        for k, parts in enumerate((key_grads, value_grads)):
            parts += [total[h, k] for h in range(heads)]
    return (*outs, jnp.concatenate(key_grads, 1), jnp.concatenate(value_grads, 1))


def by_heads(queries, keys, values, output_gradient):
    tp = lax.axis_size("tp")
    ctx = lax.axis_size("ctx")

    def gathered(x):
        return lax.all_to_all(x, "tp", split_axis=1, concat_axis=0, tiled=True)

    def returned(x):
        return lax.all_to_all(x, "tp", split_axis=0, concat_axis=1, tiled=True)

    queries, keys, values, grads = map(gathered, (queries, keys, values, output_gradient))
    rows = queries.shape[0]
    kv_heads = keys.shape[1] // HEAD_SIZE
    tail = head_parts(keys[rows - WINDOW_LENGTH :], values[rows - WINDOW_LENGTH :], 0, kv_heads)
    rim = lax.ppermute(tail, "ctx", [(i, i + 1) for i in range(ctx - 1)])
    absent = jnp.where(lax.axis_index("ctx") == 0, WINDOW_LENGTH, 0).astype(jnp.int32)
    both = jnp.concatenate([rim, head_parts(keys, values, 0, kv_heads)], 2)
    both_grads = jnp.zeros(both.shape, jnp.float32)
    outs, query_grads = [], []
    for start in range(0, rows, BLOCK):
        here = slice(start, start + BLOCK)
        before = [both[:, :, at : at + BLOCK] for at in range(start, start + WINDOW_LENGTH, BLOCK)]
        o, dq, *parts = attention(
            jnp.maximum(absent - start, 0).reshape(1), queries[here], grads[here], keys[here], values[here],
            before, 0, kv_heads, None,
        )
        outs.append(o)
        query_grads.append(dq)
        for n, x in enumerate(parts):
            at = start + n * BLOCK
            both_grads = both_grads.at[:, :, at : at + BLOCK].add(wide(x))
    back = lax.ppermute(both_grads[:, :, :WINDOW_LENGTH], "ctx", [(i + 1, i) for i in range(ctx - 1)])
    own = both_grads[:, :, WINDOW_LENGTH:]
    own = own.at[:, :, rows - WINDOW_LENGTH :].add(back).astype(jnp.bfloat16)
    results = (jnp.concatenate(outs), jnp.concatenate(query_grads), side_by_side(own[:, 0]), side_by_side(own[:, 1]))
    return tuple(map(returned, results))


def on_device(queries, keys, values, output_gradient):
    rows = queries.shape[0]
    if 2 * rows == WINDOW_LENGTH and lax.axis_size(AXES) % 2 == 0:
        return by_tokens(queries, keys, values, output_gradient)
    return by_heads(queries, keys, values, output_gradient)


def solution(mesh):
    spec = P(AXES, None)
    return jax.shard_map(
        on_device, mesh=mesh, in_specs=(spec,) * 4, out_specs=(spec,) * 4, check_vma=False
    )
```
